32 devices in a mesh: client: 16 (over z, y, core), mp: 2 (over x).
Axes of the slice: x: 2, y: 2, z: 4, core: 2. Of those that a mesh axis runs over, the one named last changes fastest.
Arguments:
- hidden: bfloat16 [16, 4, 128, 7168], P('client', None, None, 'mp'), may hold values from -6 to 6
- weight: bfloat16 [16, 7168, 2048], P('client', 'mp'), may hold values from -0.0625 to 0.0625
- target: bfloat16 [16, 4, 128, 2048], P('client', None, 'mp'), may hold values from -6 to 6
- router_prob: float32 [16, 4, 128], P('client', None, 'mp'), may hold values from 0.2 to 1
- routes: int32 [16, 4, 128, 2], P('client', None, 'mp'), may hold values from 0 to 7, all different within a row
- assign: int32 [16, 1], replicated, may hold values from 0 to 3
Outputs:
- merged_weight: bfloat16 [16, 7168, 2048], P('client', 'mp')
The draws below stay inside these ranges and needn't reach their ends.
Inputs may be any that keep to these rules, and one draw needn't show every extreme that they name: `routes`: each token names two different experts; the given weights are those of expert 0. `assign`: every cluster has at least one client.
All inputs are finite; a program needn't handle non-finite values.
Results may differ from the reference program's by a relative error of at most 0.0044.
The reference program's roundings to bfloat16 on the way (of `grad_out`, `a_weight` and `merged`) count: a program that leaves them out, or rounds other values in their place, can miss the bound.
Values may be sent and summed in bfloat16 or wider, within the bound.
No kernel may reach another device: no remote copies, remote signals or barrier semaphores. Data moves between devices by JAX's collectives and lax.ppermute only.
A program may use at most 256 MiB of HBM per device.

```python
import jax
import jax.numpy as jnp
from jax import lax

D = 2048
FFW = 7168
EXPERTS = 8
NB = 4
TOKB = 128
CLUSTERS = 4
CLIENTS = 16


def shard_levels(stream_key, shape, pieces, low, largest):
    def one(dim, parts):
        draws = jax.random.uniform(jax.random.fold_in(jax.random.fold_in(stream_key, 6), dim), (parts,), jnp.float32, low / len(pieces), largest / len(pieces))
        return jnp.repeat(jnp.exp(draws), shape[dim] // parts).reshape((-1,) + (1,) * (len(shape) - dim - 1))

    gain = one(*pieces[0])
    for cut in pieces[1:]:
        gain = gain * one(*cut)
    return gain


def picks_of(rng, rows, amount, top, lift):
    ranking = jax.random.permutation(jax.random.fold_in(rng, 1), amount)
    boost = ranking
    for power in range(3):
        boost = boost * boost // amount
    boost = boost * lift // amount
    tickets = jax.random.randint(jax.random.fold_in(rng, 2), (rows, amount), 0, 4096) + boost
    fixed_rows = jax.random.permutation(jax.random.fold_in(rng, 3), rows)[jnp.arange(amount) % rows]
    tickets = jnp.where(jnp.arange(rows)[:, None] == fixed_rows[None, :], 1 << 14, tickets)
    merit = tickets * amount + jnp.arange(amount)
    return lax.top_k(merit.astype(jnp.int32), top)[1].astype(jnp.int32)


def bell_draw(rng, extent, scale, bound, split=(), held_as=jnp.bfloat16):
    array = scale * jax.random.normal(rng, extent, jnp.float32)
    if split:
        array = array * shard_levels(rng, extent, split, -0.22, 0.18)
    return jnp.clip(array, -bound, bound).astype(held_as)


def setup_inputs(seed: int = 0) -> dict:
    key_list = jax.random.split(jax.random.key(seed), 7)
    return {
        "hidden": bell_draw(key_list[0], (CLIENTS, NB, TOKB, FFW), 1.0, 6.0, ((0, 16), (3, 2))),
        "weight": bell_draw(key_list[1], (CLIENTS, FFW, D), FFW ** -0.5, 0.0625, ((0, 16), (1, 2))),
        "target": bell_draw(key_list[2], (CLIENTS, NB, TOKB, D), 1.0, 6.0, ((0, 16), (2, 2))),
        "router_prob": jnp.clip(0.2 + 0.8 * jax.random.uniform(key_list[3], (CLIENTS, NB, TOKB), jnp.float32) ** shard_levels(key_list[3], (CLIENTS, NB, TOKB), ((0, 16), (2, 2)), -0.2, 0.2), 0.2, 1.0),
        "routes": picks_of(key_list[4], CLIENTS * NB * TOKB, EXPERTS, 2, 4096).reshape((CLIENTS, NB, TOKB, 2)),
        "assign": picks_of(key_list[5], CLIENTS, CLUSTERS, 1, 2048),
    }


EPS = 1e-6
FLOOR = 0.1


def client_fisher(hid, wgt, tgt, prob, rts):
    fisher = jnp.zeros((FFW, D), jnp.float32)
    for batch in range(NB):
        outputs = jnp.dot(hid[batch], wgt, preferred_element_type=jnp.float32)
        token_weight = jnp.where(jnp.any(rts[batch] == 0, axis=-1), prob[batch], 0.0).astype(jnp.float32)
        grad_out = (token_weight[:, None] * (outputs - tgt[batch].astype(jnp.float32))).astype(jnp.bfloat16)
        grad = jnp.dot(hid[batch].T, grad_out, preferred_element_type=jnp.float32)
        fisher = fisher + grad * grad
    return fisher


def reference(hidden, weight, target, router_prob, routes, assign):
    def accumulate(carry, items):
        num_acc, den_acc = carry
        hid, wgt, tgt, prob, rts, cluster = items
        fisher = client_fisher(hid, wgt, tgt, prob, rts)
        mean_fisher = jnp.sum(fisher) / (FFW * D)
        a_weight = (fisher / (mean_fisher + EPS) + FLOOR).astype(jnp.bfloat16)
        a_float = a_weight.astype(jnp.float32)
        num_acc = num_acc.at[cluster[0]].add(a_float * wgt.astype(jnp.float32))
        den_acc = den_acc.at[cluster[0]].add(a_float)
        return (num_acc, den_acc), None

    start = (jnp.zeros((CLUSTERS, FFW, D), jnp.float32), jnp.zeros((CLUSTERS, FFW, D), jnp.float32))
    (num_acc, den_acc), _ = lax.scan(accumulate, start, (hidden, weight, target, router_prob, routes, assign))
    merged = (num_acc / den_acc).astype(jnp.bfloat16)
    return merged[assign[:, 0]]
```

```python
import functools

import jax
import jax.numpy as jnp
from jax import lax
from jax.experimental import pallas as pl
from jax.experimental.pallas import tpu as pltpu
from jax.sharding import PartitionSpec as P

CLUSTERS = 4
EPS = 1e-06
FLOOR = 0.1
LAYERS = 4
LEAD = 5
VMEM = 48 * 1024 * 1024
F32 = jnp.float32
BF16 = jnp.bfloat16
HUB, UPPER, COLUMN, SIDE, FIRST = range(5)


def call(kernel, grid, ids, scales, in_specs, operands, out_specs, out_shape, name, cost, **kw):
    prefetch = [ids] if scales is None else [ids, scales]
    aliases = {len(prefetch) + i: o for i, o in kw.pop("aliases", {}).items()}
    return pl.pallas_call(
        kernel,
        out_shape=out_shape,
        grid_spec=pltpu.PrefetchScalarGridSpec(
            num_scalar_prefetch=len(prefetch),
            grid=grid,
            in_specs=in_specs,
            out_specs=out_specs,
            scratch_shapes=kw.pop("scratch", []),
        ),
        input_output_aliases=aliases,
        compiler_params=pltpu.CompilerParams(vmem_limit_bytes=VMEM),
        cost_estimate=pl.CostEstimate(flops=cost[0], bytes_accessed=cost[1], transcendentals=0),
        name=name,
    )(*prefetch, *operands)


def merge_kernel(peers, parts, final, extra, ids_ref, scale_ref, *refs):
    weights, hiddens, refs = refs[: 2 * peers], refs[2 * peers : 4 * peers], refs[4 * peers :]
    grads, refs = refs[: 2 * peers * parts], refs[2 * peers * parts :]
    got_ref = refs[0] if final else None
    out_ref, num, den = refs[-3:]

    @pl.when(ids_ref[HUB] == 1)
    def _():
        if final:
            num[...] = got_ref[:CLUSTERS].astype(F32)
            den[...] = got_ref[CLUSTERS:].astype(F32)
        else:
            num[...] = jnp.zeros_like(num)
            den[...] = jnp.zeros_like(den)
        tokens = hiddens[0].shape[1] // 4
        for slot in range(2 * peers):
            fisher = None
            for batch in range(4):
                part, start = divmod(batch * tokens, grads[0].shape[0])
                grad = jnp.dot(
                    hiddens[slot][:, batch * tokens : (batch + 1) * tokens],
                    grads[slot * parts + part][start : start + tokens, :],
                    preferred_element_type=F32,
                )
                fisher = grad * grad if fisher is None else fisher + grad * grad
            a_weight = (fisher * scale_ref[slot] + FLOOR).astype(BF16).astype(F32)
            cluster = ids_ref[FIRST + slot]
            num[cluster] += a_weight * weights[slot][...].astype(F32)
            den[cluster] += a_weight
        if final:
            out_ref[...] = (num[...] / den[...]).astype(BF16)
        else:
            out_ref[:CLUSTERS] = num[...].astype(BF16)
            out_ref[CLUSTERS:] = den[...].astype(BF16)


def merge_step(ids, scales, chunk, grads, rows, half, got, planes, held, after):
    final = got is not None
    peers = len(grads) // 2
    parts = len(grads[0])
    tokens = sum(array.shape[1] for array, _ in grads[0])
    width = 256 if half % 256 == 0 else half
    tiles = half // width
    in_specs, operands = [], []
    for (array, index), row, offset in chunk["weights"]:
        operands.append(array)
        in_specs.append(
            pl.BlockSpec(
                (None, rows, width),
                lambda g, ids, sc, i=index, row=row, first=offset // width: (
                    i,
                    row,
                    first + ids[SIDE] * tiles + g,
                ),
            )
        )
    for (array, index), row in chunk["hiddens"]:
        operands.append(array)
        in_specs.append(
            pl.BlockSpec((None, rows, tokens), lambda g, ids, sc, i=index, row=row: (i, row, 0))
        )
    for slot in grads:
        for array, index in slot:
            operands.append(array)
            in_specs.append(
                pl.BlockSpec(
                    (None, array.shape[1], width),
                    lambda g, ids, sc, index=index: (index, 0, ids[SIDE] * tiles + g),
                )
            )
    if final:
        operands.append(got)
        in_specs.append(pl.BlockSpec((2 * CLUSTERS, rows, width), lambda g, ids, sc: (0, 0, g)))
    aliases = {}
    if held is not None:
        aliases = {len(operands): 0}
        operands.append(held)
        in_specs.append(pl.BlockSpec(memory_space=pl.ANY))
    for array in after:
        operands.append(array)
        in_specs.append(pl.BlockSpec(memory_space=pl.ANY))
    if final:
        place = planes // CLUSTERS - 1
        out_spec = pl.BlockSpec((CLUSTERS, rows, width), lambda g, ids, sc: (place, 0, g))
    else:
        out_spec = pl.BlockSpec((2 * CLUSTERS, rows, width), lambda g, ids, sc: (0, 0, g))
    return call(
        functools.partial(merge_kernel, peers, parts, final, len(after)),
        (tiles,),
        ids,
        scales,
        in_specs,
        operands,
        out_spec,
        jax.ShapeDtypeStruct((planes, rows, half), BF16),
        "merge_final" if final else "merge_partial",
        (4 * peers * rows * tokens * half, 4 * peers * (rows * half + rows * tokens + tokens * half)),
        aliases=aliases,
        scratch=[pltpu.VMEM((CLUSTERS, rows, width), F32)] * 2,
    )


def planes_spec(array, rows, half):
    last = array.shape[0] // CLUSTERS - 1
    return pl.BlockSpec((CLUSTERS, rows, half), lambda *_: (last, 0, 0))


def pack_kernel(up, ids_ref, mine_ref, other_ref, *refs):
    out_ref = refs[-1]
    half = mine_ref.shape[2]
    base = out_ref.shape[2] - 2 * half

    @pl.when((ids_ref[HUB] == 1) & (ids_ref[UPPER] == 0))
    def _():
        out_ref[:CLUSTERS, :, base : base + half] = other_ref[...]
        out_ref[:CLUSTERS, :, base + half :] = mine_ref[...]

    @pl.when((ids_ref[HUB] == 1) & (ids_ref[UPPER] == 1))
    def _():
        out_ref[:CLUSTERS, :, base : base + half] = mine_ref[...]
        out_ref[:CLUSTERS, :, base + half :] = other_ref[...]

    if up:

        @pl.when(ids_ref[HUB] == 0)
        def _():
            for peer, ref in enumerate(refs[:-1]):
                out_ref[peer] = ref[...]


def pack_step(ids, mine, other, source, row, rows, half, peers):
    in_specs = [planes_spec(mine, rows, half), planes_spec(other, rows, half)]
    operands = [mine, other]
    width = 2 * half
    for array, index in source:
        width = array.shape[2]
        in_specs.append(pl.BlockSpec((None, rows, width), lambda g, ids, i=index: (i, row, 0)))
        operands.append(array)
    shape = (max(peers, CLUSTERS), rows, width)
    return call(
        functools.partial(pack_kernel, bool(source)),
        (1,),
        ids,
        None,
        in_specs,
        operands,
        pl.BlockSpec(shape, lambda g, ids: (0, 0, 0)),
        jax.ShapeDtypeStruct(shape, BF16),
        "pack",
        (0, 4 * shape[0] * rows * width),
    )


def pick_kernel(peers, chunks, ids_ref, *refs):
    outs = refs[-2:]
    for index in range(chunks):
        mine_ref, other_ref, leaf_ref = refs[3 * index : 3 * index + 3]
        half = mine_ref.shape[2]
        base = leaf_ref.shape[2] - 2 * half
        for peer in range(peers):
            cluster = ids_ref[FIRST + peer]
            out_ref = outs[peer // (peers // 2)]
            to = peer % (peers // 2)

            @pl.when((ids_ref[HUB] == 1) & (ids_ref[UPPER] == 0))
            def _():
                out_ref[to, index, :, :half] = other_ref[cluster]
                out_ref[to, index, :, half:] = mine_ref[cluster]

            @pl.when((ids_ref[HUB] == 1) & (ids_ref[UPPER] == 1))
            def _():
                out_ref[to, index, :, :half] = mine_ref[cluster]
                out_ref[to, index, :, half:] = other_ref[cluster]

            @pl.when(ids_ref[HUB] == 0)
            def _():
                out_ref[to, index] = leaf_ref[cluster, :, base:]


def pick_step(ids, group, rows, half, peers):
    in_specs, operands = [], []
    for mine, other, leaf in group:
        operands += [mine, other, leaf]
        in_specs += [planes_spec(mine, rows, half), planes_spec(other, rows, half)]
        in_specs.append(pl.BlockSpec(leaf.shape, lambda *_: (0, 0, 0)))
    shape = (peers // 2, len(group), rows, 2 * half)
    return call(
        functools.partial(pick_kernel, peers, len(group)),
        (1,),
        ids,
        None,
        in_specs,
        operands,
        [pl.BlockSpec(shape, lambda g, ids: (0, 0, 0, 0))] * 2,
        [jax.ShapeDtypeStruct(shape, BF16)] * 2,
        "pick",
        (0, 16 * rows * half * len(group) * peers),
    )


def place_kernel(peers, ids_ref, *refs):
    out_ref, token_ref = refs[-2:]
    token_ref[...] = jnp.zeros_like(token_ref)
    for peer in range(peers):

        @pl.when(pl.program_id(1) == peer)
        def _(peer=peer):
            out_ref[...] = refs[peer][...]


def place_step(ids, blocks, result):
    peers = len(blocks)
    _, chunks, rows, width = blocks[0][0].shape
    step = 1 + peers
    in_specs = [
        pl.BlockSpec((None, None, rows, width), lambda c, p, ids, i=index: (i, c, 0, 0))
        for _, index in blocks
    ]
    return call(
        functools.partial(place_kernel, peers),
        (chunks, peers),
        ids,
        None,
        in_specs + [pl.BlockSpec(memory_space=pl.ANY)],
        [array for array, _ in blocks] + [result],
        [
            pl.BlockSpec((rows, width), lambda c, p, ids: (ids[c * step + 1 + p], ids[c * step])),
            pl.BlockSpec((8, 128), lambda c, p, ids: (0, 0)),
        ],
        [jax.ShapeDtypeStruct(result.shape, BF16), jax.ShapeDtypeStruct((8, 128), F32)],
        "place",
        (0, 4 * chunks * peers * rows * width),
        aliases={peers: 0},
    )


def forward_kernel(own, batches, ids_ref, hidden_ref, weight_ref, target_ref, *outs):
    total = jnp.dot(hidden_ref[...], weight_ref[...], preferred_element_type=F32)
    tokens = hidden_ref.shape[0] // batches
    span = target_ref.shape[1]
    half = batches // 2
    for part in range(2):
        out_ref = outs[part]
        out_ref[...] = total[part * half * tokens : (part + 1) * half * tokens]
        for batch in range(half):
            rows = pl.ds(pl.multiple_of(batch * tokens + ids_ref[0] * span, 8), span)
            out_ref[rows, :] = out_ref[rows, :] - target_ref[part * half + batch].astype(F32)
    if own:

        @pl.when(pl.program_id(0) == 0)
        def _():
            for batch in range(batches):
                rows = hidden_ref[batch * tokens : (batch + 1) * tokens, :]
                outs[2][batch] = lax.dot_general(
                    rows, rows, (((1,), (1,)), ((), ())), preferred_element_type=F32
                )


def forward_step(ids, flat, weight, target, block, shards, own):
    every, depth = flat.shape
    batches = target.shape[0]
    tokens = every // batches
    width = min(block, 256)
    tiles = block // width
    count = tiles if own else tiles * (shards - 1)
    columns = lambda g, ids: ids[1 + g // tiles] * tiles + g % tiles
    out_specs = [pl.BlockSpec((every // 2, width), lambda g, ids: (0, g))] * 2
    out_shape = [jax.ShapeDtypeStruct((every // 2, count * width), F32)] * 2
    if own:
        out_specs.append(pl.BlockSpec((batches, tokens, tokens), lambda g, ids: (0, 0, 0)))
        out_shape.append(jax.ShapeDtypeStruct((batches, tokens, tokens), F32))
    return call(
        functools.partial(forward_kernel, own, batches),
        (count,),
        ids.astype(jnp.int32),
        None,
        [
            pl.BlockSpec((every, depth), lambda g, ids: (0, 0)),
            pl.BlockSpec((depth, width), lambda g, ids: (0, columns(g, ids))),
            pl.BlockSpec((batches, target.shape[1], width), lambda g, ids: (0, 0, columns(g, ids))),
        ],
        [flat, weight, target],
        out_specs,
        out_shape,
        "forward",
        (2 * every * depth * count * width, 2 * depth * (every + count * width)),
    )


def cut_kernel(count, every, ids_ref, weight_ref, *refs):
    outs = refs[-2:]
    for index in range(2):

        @pl.when(pl.program_id(0) // count == index)
        def _(index=index):
            if every:
                outs[index][:, :every] = refs[0][...]
            outs[index][:, every:] = weight_ref[...]


def cut_step(ids, weight, turned, size, chunks, block, peers, after):
    count = peers // 2
    in_specs = [pl.BlockSpec((size, block), lambda p, c, ids: (ids[1 + p] + c, ids[0]))]
    operands = [weight]
    every = 0
    if turned is not None:
        every = turned.shape[1]
        in_specs.append(pl.BlockSpec((size, every), lambda p, c, ids: (ids[1 + p] + c, 0)))
        operands.append(turned)
    for array in after:
        operands.append(array)
        in_specs.append(pl.BlockSpec(memory_space=pl.ANY))
    shape = (count, chunks * size, every + block)
    spec = lambda index: pl.BlockSpec((None, size, every + block), index)
    return call(
        functools.partial(cut_kernel, count, every),
        (peers, chunks),
        ids,
        None,
        in_specs,
        operands,
        [
            spec(lambda p, c, ids: (jnp.minimum(p, count - 1), jnp.where(p < count, c, chunks - 1), 0)),
            spec(lambda p, c, ids: (jnp.maximum(p - count, 0), jnp.where(p < count, 0, c), 0)),
        ],
        [jax.ShapeDtypeStruct(shape, BF16)] * 2,
        "cut",
        (0, 8 * count * shape[1] * shape[2]),
    )


def body(clients, shards, hidden, weight, target, router_prob, routes, assign):
    batches, tokens, depth = hidden.shape[1:]
    width = weight.shape[2]
    peers = clients // LAYERS
    rows = depth // peers
    block = width // shards
    half = block // 2
    pieces = max(1, 14 // shards)
    if rows % (16 * pieces):
        pieces = 1
    size = rows // pieces
    every = batches * tokens
    chunks = [(j, r) for j in range(shards) for r in range(pieces)]
    count = len(chunks)
    lead = min(LEAD, count)

    client = lax.axis_index("client")
    shard = lax.axis_index("mp")
    layer, place = client // peers, client % peers
    is_hub = (layer == 1) | (layer == 2)
    upper = (layer >= 2).astype(jnp.int32)
    ranks = place ^ jnp.arange(peers)

    def swap(k):
        return [(z * peers + q, z * peers + (q ^ k)) for z in range(LAYERS) for q in range(peers)]

    def between(links):
        return [(a * peers + q, b * peers + q) for a, b in links for q in range(peers)]

    to_peer = lambda array, k: lax.ppermute(array, "client", swap(k))
    leaf_to_hub = lambda array: lax.ppermute(array, "client", between([(0, 1), (3, 2)]))
    leaf_and_hub = lambda array: lax.ppermute(
        array, "client", between([(0, 1), (1, 0), (2, 3), (3, 2)])
    )
    hub_to_hub = lambda array: lax.ppermute(array, "client", between([(1, 2), (2, 1)]))
    ahead = lambda j: [(s, (s + j) % shards) for s in range(shards)]
    behind = lambda j: [(s, (s - j) % shards) for s in range(shards)]

    def exchange(held):
        held = list(held)
        bit = peers // 2
        while bit:
            moved = [k for k in range(peers) if k & bit]
            arrays = {id(held[k][0]) for k in moved}
            if len(arrays) == 1 and held[moved[0]][0].shape[0] == len(moved):
                array = held[moved[0]][0]
            else:
                array = jnp.stack([held[k][0][held[k][1]] for k in moved])
            got = to_peer(array, bit)
            for i, k in enumerate(moved):
                held[k] = (got, i)
            bit //= 2
        return held

    def gather_peers(arrays):
        held = [{0: (array[None], 0)} for array in arrays]
        bit = peers // 2
        while bit:
            keys = [(n, k) for n in range(len(held)) for k in held[n]]
            if bit == peers // 2:
                for n, k in keys:
                    array, i = held[n][k]
                    held[n][k ^ bit] = (to_peer(array[i][None], bit), 0)
            else:
                got = to_peer(jnp.stack([held[n][k][0][held[n][k][1]] for n, k in keys]), bit)
                for i, (n, k) in enumerate(keys):
                    held[n][k ^ bit] = (got, i)
            bit //= 2
        return [[h[k] for k in range(peers)] for h in held]

    local_weight = weight[0]
    flat = hidden[0].reshape(every, depth)
    turned = flat.T
    others_at = jnp.concatenate([shard[None], (shard + jnp.arange(1, shards)) % shards])
    others = forward_step(others_at, flat, local_weight, target[0], block, shards, False)
    mine_at = jnp.stack([shard, shard])
    *mine, hidden_gram = forward_step(mine_at, flat, local_weight, target[0], block, shards, True)
    hidden_gram = lax.psum(hidden_gram, "mp")
    token_weight = jnp.where(jnp.any(routes[0] == 0, axis=-1), router_prob[0], 0.0)
    token_weight = jnp.stack(
        [token_weight] + [lax.ppermute(token_weight, "mp", behind(j)) for j in range(1, shards)]
    )
    token_weight = token_weight[(jnp.arange(shards) - shard) % shards]
    token_weight = token_weight.transpose(1, 0, 2).reshape(every, 1)
    grad_parts = []
    for part in range(2):
        total = mine[part]
        for j in range(1, shards):
            total = total + lax.ppermute(
                others[part][:, (j - 1) * block : j * block], "mp", ahead(j)
            )
        grad = token_weight[part * every // 2 : (part + 1) * every // 2] * total
        grad_parts.append(grad.astype(BF16))

    def spread_grads(parts):
        many = [gather_peers([part, leaf_to_hub(part)]) for part in parts]
        return [[many[p][side][k] for p in range(len(parts))] for side in range(2) for k in range(peers)]

    grads = {0: spread_grads(grad_parts)}

    gram = sum(
        jnp.sum(
            hidden_gram[part * batches // 2 : (part + 1) * batches // 2]
            * jnp.einsum(
                "btd,bsd->bts", *[g.reshape(batches // 2, tokens, block)] * 2, preferred_element_type=F32
            )
        )
        for part, g in enumerate(grad_parts)
    )
    gram = jnp.full((8, 128), gram)
    total = gram
    for j in range(1, shards):
        total = total + lax.ppermute(gram, "mp", ahead(j))
    totals = [a[i, 0, 0] for side in gather_peers([total, leaf_to_hub(total)]) for a, i in side]
    scales = 1.0 / (jnp.stack(totals) / (depth * shards * width) + EPS)

    cluster_of = assign[:, 0].astype(jnp.int32)
    slot_clients = jnp.concatenate(
        [layer * peers + ranks, jnp.where(upper == 1, 3, 0) * peers + ranks]
    )
    slot_clusters = cluster_of[slot_clients]

    own, far = {}, {}

    def spread(j, low, high, after):
        order = [place ^ (k + peers // 2) % peers for k in range(peers)]
        at = jnp.stack([(shard + j) % shards] + [q * pieces + low for q in order]).astype(jnp.int32)
        hi, lo = cut_step(
            at, local_weight, None if j else turned, size, high - low, block, peers, after
        )
        parts = peers // 2
        held = exchange([((lo, hi)[k // parts], k % parts) for k in range(peers)])
        numbers = [j * pieces + r for r in range(low, high)]
        for i, c in enumerate(numbers):
            own[c] = (held, i)
        early = sum(c < lead for c in numbers)
        if early:
            array = leaf_to_hub(jnp.stack([a[i, : early * size] for a, i in held]))
            for i in range(early):
                far[numbers[i]] = ([(array, k) for k in range(peers)], i)
        return held[-1][0]

    if pieces > 3:
        spread(0, 0, 1, [])
        spread(0, 1, 3, [others[0]])
        last = spread(0, 3, pieces, [grads[0][peers // 2][1][0]])
    else:
        last = spread(0, 0, pieces, [])
        for j in range(1, shards):
            last = spread(j, 0, pieces, [last])

    def ids_for(c, side):
        head = [is_hub, upper, (shard + chunks[c][0]) % shards, side]
        return jnp.concatenate([jnp.stack([v.astype(jnp.int32) for v in head]), slot_clusters])

    def merge(c, side, got, planes, held, after=()):
        j, r = chunks[c]
        weights, hiddens = [], []
        for table in (own, far):
            slots, row = table[c]
            weights += [(slot, row, 0 if j else every) for slot in slots]
            slots, row = table[r]
            hiddens += [(slot, row) for slot in slots]
        chunk = dict(weights=weights, hiddens=hiddens)
        return merge_step(
            ids_for(c, side), scales, chunk, grads[j], size, half, got, planes, held, after
        )

    result = jnp.zeros((depth, width), BF16)
    sent, got, leaf, tokens_of = {}, {}, {}, {}
    waiting = []

    def finish(c):
        nonlocal result, waiting
        later = c + lead
        source, row = own[later] if later < count else ([], 0)
        packed = pack_step(
            ids_for(c, upper), sent[c + 2], got[c + 2], source, row, size, half, peers
        )
        leaf[c] = leaf_and_hub(packed)
        if later < count:
            far[later] = ([(leaf[c], k) for k in range(peers)], 0)
        waiting.append(c)
        if len(waiting) == 2 or c >= count - 2:
            lo, hi = pick_step(
                ids_for(c, upper),
                [(sent[w + 2], got[w + 2], leaf[w]) for w in waiting],
                size,
                half,
                peers,
            )
            parts = peers // 2
            held = exchange([((lo, hi)[k // parts], k % parts) for k in range(peers)])
            where = []
            for w in waiting:
                where.append(((shard + chunks[w][0]) % shards)[None])
                where.append(ranks * pieces + chunks[w][1])
            result, token = place_step(jnp.concatenate(where).astype(jnp.int32), held, result)
            for w in waiting:
                tokens_of[w] = token
            waiting = []

    for t in range(count + 2):
        if t >= 3:
            finish(t - 3)
        planes = (2 if t < count else 0) * CLUSTERS + (CLUSTERS if t >= 2 else 0)
        buffer = None
        if t >= 2:
            buffer = merge(t - 2, 1 - upper, got[t - 2], planes, None)
        if t < count:
            after = []
            if t - 6 in leaf:
                after.append(leaf[t - 6])
            if t - 8 in tokens_of:
                after.append(tokens_of[t - 8])
            buffer = merge(t, upper, None, planes, buffer, after)
        sent[t] = buffer
        got[t] = hub_to_hub(buffer)
        j = 1 + t * (shards - 1) // max(1, pieces * (shards - 1))
        if t % pieces == 0 and j < shards and pieces > 3:
            last = spread(j, 0, pieces, [last, got[t]])
        if t % pieces == min(2, pieces - 1) and j < shards:
            grads[j] = spread_grads([lax.ppermute(g, "mp", behind(j)) for g in grad_parts])
    finish(count - 1)
    return result[None]


def solution(mesh):
    placed = (
        P("client", None, None, "mp"),
        P("client", "mp", None),
        P("client", None, "mp", None),
        P("client", None, "mp"),
        P("client", None, "mp", None),
        P(),
    )
    return jax.shard_map(
        functools.partial(body, mesh.shape["client"], mesh.shape["mp"]),
        mesh=mesh,
        in_specs=placed,
        out_specs=P("client", "mp", None),
        check_vma=False,
    )
```

```python
import functools

import jax
import jax.numpy as jnp
from jax import lax
from jax.experimental import pallas as pl
from jax.experimental.pallas import tpu as pltpu
from jax.sharding import PartitionSpec as P

CLUSTERS = 4
EPS = 1e-06
FLOOR = 0.1
LAYERS = 4
LEAD = 7
VMEM = 48 * 1024 * 1024
F32 = jnp.float32
BF16 = jnp.bfloat16
HUB, UPPER, COLUMN, SIDE, FIRST = range(5)


def call(kernel, grid, ids, scales, in_specs, operands, out_specs, out_shape, name, cost, **kw):
    prefetch = [ids] if scales is None else [ids, scales]
    aliases = {len(prefetch) + i: o for i, o in kw.pop("aliases", {}).items()}
    return pl.pallas_call(
        kernel,
        out_shape=out_shape,
        grid_spec=pltpu.PrefetchScalarGridSpec(
            num_scalar_prefetch=len(prefetch),
            grid=grid,
            in_specs=in_specs,
            out_specs=out_specs,
            scratch_shapes=kw.pop("scratch", []),
        ),
        input_output_aliases=aliases,
        compiler_params=pltpu.CompilerParams(vmem_limit_bytes=VMEM),
        cost_estimate=pl.CostEstimate(flops=cost[0], bytes_accessed=cost[1], transcendentals=0),
        name=name,
    )(*prefetch, *operands)


def gate(value, after):
    anywhere = pl.BlockSpec(memory_space=pl.ANY)
    return pl.pallas_call(
        lambda *refs: None,
        out_shape=jax.ShapeDtypeStruct(value.shape, value.dtype),
        in_specs=[anywhere] * (1 + len(after)),
        out_specs=anywhere,
        input_output_aliases={0: 0},
        cost_estimate=pl.CostEstimate(flops=1, bytes_accessed=1, transcendentals=0),
        name="gate",
    )(value, *after)


def merge_kernel(peers, parts, final, extra, ids_ref, scale_ref, *refs):
    weights, hiddens, refs = refs[: 2 * peers], refs[2 * peers : 4 * peers], refs[4 * peers :]
    grads, refs = refs[: 2 * peers * parts], refs[2 * peers * parts :]
    got_ref = refs[0] if final else None
    out_ref, num, den = refs[-3:]

    @pl.when(ids_ref[HUB] == 1)
    def _():
        if final:
            num[...] = got_ref[:CLUSTERS].astype(F32)
            den[...] = got_ref[CLUSTERS:].astype(F32)
        else:
            num[...] = jnp.zeros_like(num)
            den[...] = jnp.zeros_like(den)
        tokens = hiddens[0].shape[1] // 4
        for slot in range(2 * peers):
            fisher = None
            for batch in range(4):
                part, start = divmod(batch * tokens, grads[0].shape[0])
                grad = jnp.dot(
                    hiddens[slot][:, batch * tokens : (batch + 1) * tokens],
                    grads[slot * parts + part][start : start + tokens, :],
                    preferred_element_type=F32,
                )
                fisher = grad * grad if fisher is None else fisher + grad * grad
            a_weight = (fisher * scale_ref[slot] + FLOOR).astype(BF16).astype(F32)
            cluster = ids_ref[FIRST + slot]
            num[cluster] += a_weight * weights[slot][...].astype(F32)
            den[cluster] += a_weight
        if final:
            out_ref[...] = (num[...] / den[...]).astype(BF16)
        else:
            out_ref[:CLUSTERS] = num[...].astype(BF16)
            out_ref[CLUSTERS:] = den[...].astype(BF16)


def merge_step(ids, scales, chunk, grads, rows, half, got, planes, held, after):
    final = got is not None
    peers = len(grads) // 2
    parts = len(grads[0])
    tokens = sum(array.shape[1] for array, _ in grads[0])
    width = 256 if half % 256 == 0 else half
    tiles = half // width
    in_specs, operands = [], []
    for (array, index), row, offset in chunk["weights"]:
        operands.append(array)
        in_specs.append(
            pl.BlockSpec(
                (None, rows, width),
                lambda g, ids, sc, i=index, row=row, first=offset // width: (
                    i,
                    row,
                    first + ids[SIDE] * tiles + g,
                ),
            )
        )
    for (array, index), row in chunk["hiddens"]:
        operands.append(array)
        in_specs.append(
            pl.BlockSpec((None, rows, tokens), lambda g, ids, sc, i=index, row=row: (i, row, 0))
        )
    for slot in grads:
        for array, index in slot:
            operands.append(array)
            in_specs.append(
                pl.BlockSpec(
                    (None, array.shape[1], width),
                    lambda g, ids, sc, index=index: (index, 0, ids[SIDE] * tiles + g),
                )
            )
    if final:
        operands.append(got)
        in_specs.append(pl.BlockSpec((2 * CLUSTERS, rows, width), lambda g, ids, sc: (0, 0, g)))
    aliases = {}
    if held is not None:
        aliases = {len(operands): 0}
        operands.append(held)
        in_specs.append(pl.BlockSpec(memory_space=pl.ANY))
    for array in after:
        operands.append(array)
        in_specs.append(pl.BlockSpec(memory_space=pl.ANY))
    if final:
        place = planes // CLUSTERS - 1
        out_spec = pl.BlockSpec((CLUSTERS, rows, width), lambda g, ids, sc: (place, 0, g))
    else:
        out_spec = pl.BlockSpec((2 * CLUSTERS, rows, width), lambda g, ids, sc: (0, 0, g))
    return call(
        functools.partial(merge_kernel, peers, parts, final, len(after)),
        (tiles,),
        ids,
        scales,
        in_specs,
        operands,
        out_spec,
        jax.ShapeDtypeStruct((planes, rows, half), BF16),
        "merge_final" if final else "merge_partial",
        (4 * peers * rows * tokens * half, 4 * peers * (rows * half + rows * tokens + tokens * half)),
        aliases=aliases,
        scratch=[pltpu.VMEM((CLUSTERS, rows, width), F32)] * 2,
    )


def planes_spec(array, rows, half):
    last = array.shape[0] // CLUSTERS - 1
    return pl.BlockSpec((CLUSTERS, rows, half), lambda *_: (last, 0, 0))


def pack_kernel(up, ids_ref, mine_ref, other_ref, *refs):
    out_ref = refs[-1]
    half = mine_ref.shape[2]
    base = out_ref.shape[2] - 2 * half

    @pl.when((ids_ref[HUB] == 1) & (ids_ref[UPPER] == 0))
    def _():
        out_ref[:CLUSTERS, :, base : base + half] = other_ref[...]
        out_ref[:CLUSTERS, :, base + half :] = mine_ref[...]

    @pl.when((ids_ref[HUB] == 1) & (ids_ref[UPPER] == 1))
    def _():
        out_ref[:CLUSTERS, :, base : base + half] = mine_ref[...]
        out_ref[:CLUSTERS, :, base + half :] = other_ref[...]

    if up:

        @pl.when(ids_ref[HUB] == 0)
        def _():
            for peer in range(up):
                out_ref[peer] = refs[peer][...]


def pack_step(ids, mine, other, source, row, rows, half, peers, after):
    in_specs = [planes_spec(mine, rows, half), planes_spec(other, rows, half)]
    operands = [mine, other]
    width = 2 * half
    for array, index in source:
        width = array.shape[2]
        in_specs.append(pl.BlockSpec((None, rows, width), lambda g, ids, i=index: (i, row, 0)))
        operands.append(array)
    shape = (max(peers, CLUSTERS), rows, width)
    in_specs += [pl.BlockSpec(memory_space=pl.ANY)] * len(after)
    operands += after
    return call(
        functools.partial(pack_kernel, len(source)),
        (1,),
        ids,
        None,
        in_specs,
        operands,
        pl.BlockSpec(shape, lambda g, ids: (0, 0, 0)),
        jax.ShapeDtypeStruct(shape, BF16),
        "pack",
        (0, 4 * shape[0] * rows * width),
    )


def pick_kernel(peers, chunks, ids_ref, *refs):
    outs = refs[-2:]
    for index in range(chunks):
        mine_ref, other_ref, leaf_ref = refs[3 * index : 3 * index + 3]
        half = mine_ref.shape[2]
        base = leaf_ref.shape[2] - 2 * half
        for peer in range(peers):
            cluster = ids_ref[FIRST + peer]
            out_ref = outs[peer // (peers // 2)]
            to = peer % (peers // 2)

            @pl.when((ids_ref[HUB] == 1) & (ids_ref[UPPER] == 0))
            def _():
                out_ref[to, index, :, :half] = other_ref[cluster]
                out_ref[to, index, :, half:] = mine_ref[cluster]

            @pl.when((ids_ref[HUB] == 1) & (ids_ref[UPPER] == 1))
            def _():
                out_ref[to, index, :, :half] = mine_ref[cluster]
                out_ref[to, index, :, half:] = other_ref[cluster]

            @pl.when(ids_ref[HUB] == 0)
            def _():
                out_ref[to, index] = leaf_ref[cluster, :, base:]


def pick_step(ids, group, rows, half, peers, after):
    in_specs, operands = [], []
    for mine, other, leaf in group:
        operands += [mine, other, leaf]
        in_specs += [planes_spec(mine, rows, half), planes_spec(other, rows, half)]
        in_specs.append(pl.BlockSpec(leaf.shape, lambda *_: (0, 0, 0)))
    shape = (peers // 2, len(group), rows, 2 * half)
    in_specs += [pl.BlockSpec(memory_space=pl.ANY)] * len(after)
    operands += after
    return call(
        functools.partial(pick_kernel, peers, len(group)),
        (1,),
        ids,
        None,
        in_specs,
        operands,
        [pl.BlockSpec(shape, lambda g, ids: (0, 0, 0, 0))] * 2,
        [jax.ShapeDtypeStruct(shape, BF16)] * 2,
        "pick",
        (0, 16 * rows * half * len(group) * peers),
    )


def place_kernel(peers, ids_ref, *refs):
    out_ref, token_ref = refs[-2:]
    token_ref[...] = jnp.zeros_like(token_ref)
    for peer in range(peers):

        @pl.when(pl.program_id(1) == peer)
        def _(peer=peer):
            out_ref[...] = refs[peer][...]


def place_step(ids, blocks, result, shape, after):
    peers = len(blocks)
    _, chunks, rows, width = blocks[0][0].shape
    step = 1 + peers
    in_specs = [
        pl.BlockSpec((None, None, rows, width), lambda c, p, ids, i=index: (i, c, 0, 0))
        for _, index in blocks
    ]
    return call(
        functools.partial(place_kernel, peers),
        (chunks, peers),
        ids,
        None,
        in_specs + [pl.BlockSpec(memory_space=pl.ANY)] * (len(after) + (result is not None)),
        [array for array, _ in blocks] + [result] * (result is not None) + after,
        [
            pl.BlockSpec((rows, width), lambda c, p, ids: (ids[c * step + 1 + p], ids[c * step])),
            pl.BlockSpec((8, 128), lambda c, p, ids: (0, 0)),
        ],
        [jax.ShapeDtypeStruct(shape, BF16), jax.ShapeDtypeStruct((8, 128), F32)],
        "place",
        (0, 4 * chunks * peers * rows * width),
        aliases={peers: 0} if result is not None else {},
    )


def forward_kernel(own, batches, ids_ref, hidden_ref, weight_ref, target_ref, *refs):
    outs = refs[-1:] if own else refs[-2:]
    total = jnp.dot(hidden_ref[...], weight_ref[...], preferred_element_type=F32)
    tokens = hidden_ref.shape[0] // batches
    span = target_ref.shape[1]
    outs[0][...] = total
    for batch in range(batches):
        rows = pl.ds(pl.multiple_of(batch * tokens + ids_ref[0] * span, 8), span)
        outs[0][rows, :] = outs[0][rows, :] - target_ref[batch].astype(F32)
    if not own:

        @pl.when(pl.program_id(0) == 0)
        def _():
            for batch in range(batches):
                rows = hidden_ref[batch * tokens : (batch + 1) * tokens, :]
                outs[1][batch] = lax.dot_general(
                    rows, rows, (((1,), (1,)), ((), ())), preferred_element_type=F32
                )


def forward_step(ids, flat, weight, target, block, shards, own, after=()):
    every, depth = flat.shape
    batches = target.shape[0]
    tokens = every // batches
    width = min(block, 256)
    tiles = block // width
    count = tiles if own else tiles * (shards - 1)
    columns = lambda g, ids: ids[1 + g // tiles] * tiles + g % tiles
    out_specs = [pl.BlockSpec((every, width), lambda g, ids: (0, g))]
    out_shape = [jax.ShapeDtypeStruct((every, count * width), F32)]
    if not own:
        out_specs.append(pl.BlockSpec((batches, tokens, tokens), lambda g, ids: (0, 0, 0)))
        out_shape.append(jax.ShapeDtypeStruct((batches, tokens, tokens), F32))
    return call(
        functools.partial(forward_kernel, own, batches),
        (count,),
        ids.astype(jnp.int32),
        None,
        [
            pl.BlockSpec((every, depth), lambda g, ids: (0, 0)),
            pl.BlockSpec((depth, width), lambda g, ids: (0, columns(g, ids))),
            pl.BlockSpec((batches, target.shape[1], width), lambda g, ids: (0, 0, columns(g, ids))),
        ]
        + [pl.BlockSpec(memory_space=pl.ANY)] * len(after),
        [flat, weight, target, *after],
        out_specs,
        out_shape,
        "forward",
        (1, 1),
    )


def grad_kernel(batches, ids_ref, token_ref, gram_ref, mine_ref, *refs):
    grad_ref, total_ref = refs[-2:]
    total = mine_ref[...]
    for ref in refs[:-2]:
        total = total + ref[...]
    grad_ref[...] = (token_ref[...] * total).astype(BF16)
    tokens = grad_ref.shape[0] // batches
    squares = 0.0
    for batch in range(batches):
        rows = grad_ref[batch * tokens : (batch + 1) * tokens, :]
        gram = lax.dot_general(rows, rows, (((1,), (1,)), ((), ())), preferred_element_type=F32)
        squares = squares + jnp.sum(gram_ref[batch] * gram)
    total_ref[...] = jnp.full(total_ref.shape, squares, F32)


def grad_step(ids, token_weight, hidden_gram, mine, others):
    arrays = [token_weight, hidden_gram, mine, *others]
    whole = lambda a: pl.BlockSpec(a.shape, lambda *_: (0,) * a.ndim)
    outs = [jax.ShapeDtypeStruct(mine.shape, BF16), jax.ShapeDtypeStruct((8, 128), F32)]
    return call(
        functools.partial(grad_kernel, hidden_gram.shape[0]),
        (1,),
        ids.astype(jnp.int32),
        None,
        [whole(a) for a in arrays],
        arrays,
        [whole(a) for a in outs],
        outs,
        "grad",
        (1, 1),
    )


def cut_kernel(count, every, ids_ref, weight_ref, *refs):
    outs = refs[-2:]
    for index in range(2):

        @pl.when(pl.program_id(0) // count == index)
        def _(index=index):
            if every:
                outs[index][:, :every] = refs[0][...]
            outs[index][:, every:] = weight_ref[...]


def cut_step(ids, weight, turned, size, chunks, block, peers, after):
    count = peers // 2
    in_specs = [pl.BlockSpec((size, block), lambda p, c, ids: (ids[1 + p] + c, ids[0]))]
    operands = [weight]
    every = 0
    if turned is not None:
        every = turned.shape[1]
        in_specs.append(pl.BlockSpec((size, every), lambda p, c, ids: (ids[1 + p] + c, 0)))
        operands.append(turned)
    for array in after:
        operands.append(array)
        in_specs.append(pl.BlockSpec(memory_space=pl.ANY))
    shape = (count, chunks * size, every + block)
    spec = lambda index: pl.BlockSpec((None, size, every + block), index)
    return call(
        functools.partial(cut_kernel, count, every),
        (peers, chunks),
        ids,
        None,
        in_specs,
        operands,
        [
            spec(lambda p, c, ids: (jnp.minimum(p, count - 1), jnp.where(p < count, c, chunks - 1), 0)),
            spec(lambda p, c, ids: (jnp.maximum(p - count, 0), jnp.where(p < count, 0, c), 0)),
        ],
        [jax.ShapeDtypeStruct(shape, BF16)] * 2,
        "cut",
        (1, 1),
    )


def body(clients, shards, hidden, weight, target, router_prob, routes, assign):
    batches, tokens, depth = hidden.shape[1:]
    width = weight.shape[2]
    peers = clients // LAYERS
    rows = depth // peers
    block = width // shards
    half = block // 2
    pieces = max(1, 14 // shards)
    if rows % (16 * pieces):
        pieces = 1
    size = rows // pieces
    every = batches * tokens
    chunks = [(j, r) for j in range(shards) for r in range(pieces)]
    count = len(chunks)
    lead = min(LEAD, count)

    client = lax.axis_index("client")
    shard = lax.axis_index("mp")
    layer, place = client // peers, client % peers
    is_hub = (layer == 1) | (layer == 2)
    upper = (layer >= 2).astype(jnp.int32)
    ranks = place ^ jnp.arange(peers)

    def swap(k):
        return [(z * peers + q, z * peers + (q ^ k)) for z in range(LAYERS) for q in range(peers)]

    def between(links):
        return [(a * peers + q, b * peers + q) for a, b in links for q in range(peers)]

    to_peer = lambda array, k: lax.ppermute(array, "client", swap(k))
    leaf_to_hub = lambda array: lax.ppermute(array, "client", between([(0, 1), (3, 2)]))
    leaf_and_hub = lambda array: lax.ppermute(
        array, "client", between([(0, 1), (1, 0), (2, 3), (3, 2)])
    )
    hub_to_hub = lambda array: lax.ppermute(array, "client", between([(1, 2), (2, 1)]))
    ahead = lambda j: [(s, (s + j) % shards) for s in range(shards)]
    behind = lambda j: [(s, (s - j) % shards) for s in range(shards)]

    def exchange(held, after=(), bit=peers // 2):
        held = list(held)
        while bit:
            moved = [k for k in range(peers) if k & bit]
            arrays = {id(held[k][0]) for k in moved}
            if len(arrays) == 1 and held[moved[0]][0].shape[0] == len(moved):
                array = held[moved[0]][0]
            else:
                array = jnp.stack([held[k][0][held[k][1]] for k in moved])
            got = to_peer(array, bit)
            if after and bit == peers // 2:
                got = gate(got, after)
            for i, k in enumerate(moved):
                held[k] = (got, i)
            bit //= 2
        return held

    def gather_pair(near, distant, after, last=()):
        top = peers // 2
        near_top = to_peer(near[None], top)
        distant = gate(distant, [near_top, *after])
        distant_top = to_peer(distant[None], top)
        distant_top = gate(distant_top, last) if last else distant_top
        held = [
            {0: (near[None], 0), top: (near_top, 0)},
            {0: (distant[None], 0), top: (distant_top, 0)},
        ]
        bit = top // 2
        while bit:
            keys = [(n, k) for n in range(2) for k in held[n]]
            stack = jnp.stack([held[n][k][0][held[n][k][1]] for n, k in keys])
            got = to_peer(stack, bit)
            for i, (n, k) in enumerate(keys):
                held[n][k] = (stack, i)
                held[n][k ^ bit] = (got, i)
            bit //= 2
        slots = [h[k] for h in held for k in range(peers)]
        return slots, near_top, distant_top, stack, got

    local_weight = weight[0]
    flat = hidden[0].reshape(every, depth)
    turned = flat.T
    others_at = jnp.concatenate([shard[None], (shard + jnp.arange(1, shards)) % shards])
    others, hidden_gram = forward_step(others_at, flat, local_weight, target[0], block, shards, False)
    own_gram = hidden_gram
    for j in range(1, shards):
        hidden_gram = hidden_gram + lax.ppermute(own_gram, "mp", ahead(j))

    def cut_for(j, low, high, after):
        order = [place ^ (k + peers // 2) % peers for k in range(peers)]
        at = jnp.stack([(shard + j) % shards] + [q * pieces + low for q in order]).astype(jnp.int32)
        return tuple(
            cut_step(at, local_weight, None if j else turned, size, high - low, block, peers, after)
        )

    def spread(j, low, high, after, later=()):
        hi, lo = after if type(after) is tuple else cut_for(j, low, high, after)
        parts = peers // 2
        held = exchange([((lo, hi)[k // parts], k % parts) for k in range(peers)], later)
        numbers = [j * pieces + r for r in range(low, high)]
        for i, c in enumerate(numbers):
            own[c] = (held, i)
        return held[parts][0], held[-1][0], hi

    def lift(c, after=()):
        held, row = own[c]
        array = jnp.stack([a[i, row * size : (row + 1) * size] for a, i in held])
        array = gate(array, after) if after else array
        lifts[c] = array, leaf_to_hub(array)
        far[c] = ([(lifts[c][1], k) for k in range(peers)], 0)

    lifts = {}
    own, far = {}, {}
    fine = pieces >= 7
    early = [spread(0, 0, 1 if fine else pieces, [others])]
    if fine:
        early.append(spread(0, 1, 2, [early[0][2]]))
    mine_at = jnp.stack([shard, shard])
    (mine,) = forward_step(
        mine_at, flat, local_weight, target[0], block, shards, True, [e[2] for e in early]
    )
    token_weight = jnp.where(jnp.any(routes[0] == 0, axis=-1), router_prob[0], 0.0)
    token_weight = jnp.stack(
        [token_weight] + [lax.ppermute(token_weight, "mp", behind(j)) for j in range(1, shards)]
    )
    token_weight = token_weight[(jnp.arange(shards) - shard) % shards]
    token_weight = token_weight.transpose(1, 0, 2).reshape(every, 1)
    arrived = [
        lax.ppermute(others[:, (j - 1) * block : j * block], "mp", ahead(j)) for j in range(1, shards)
    ]
    grad, squares = grad_step(
        mine_at, token_weight, hidden_gram, gate(mine, [early[-1][0]]), arrived
    )
    total = squares
    for j in range(1, shards):
        total = total + lax.ppermute(squares, "mp", ahead(j))
    leaf_total = leaf_to_hub(total)
    totals, *scalar_steps = gather_pair(total, leaf_total, [])
    totals = jnp.stack([a[i, 0, 0] for a, i in totals])
    scales = 1.0 / (totals / (depth * shards * width) + EPS)
    leaf_grad = leaf_to_hub(grad)
    lift(0, [leaf_grad, leaf_total])
    grad_slots, *grad_steps = gather_pair(
        grad, leaf_grad, [scalar_steps[1], early[0][1], early[-1][1]], [lifts[0][1]]
    )

    grads = {0: [[slot] for slot in grad_slots]}

    cluster_of = assign[:, 0].astype(jnp.int32)
    slot_clients = jnp.concatenate(
        [layer * peers + ranks, jnp.where(upper == 1, 3, 0) * peers + ranks]
    )
    slot_clusters = cluster_of[slot_clients]

    before = {t: [] for t in range(count)}

    def column_grads(j, first_after, second_after):
        first, second = grad_steps[2:]
        come = lax.ppermute(gate(first, first_after), "mp", behind(j))
        ready = gate(second, [come, *second_after])
        pair = come, lax.ppermute(ready, "mp", behind(j))
        grads[j] = [[(pair[0] if a is first else pair[1], i)] for a, i in grad_slots]
        return come, ready

    if fine:
        lift(1, [lifts[0][1]])
        before[0].append(lifts[1][0])
    else:
        last = early[0]
        for j in range(1, shards):
            last = spread(j, 0, pieces, [last[1]])
        for c in range(1, lead):
            lift(c)

    def ids_for(c, side):
        head = [is_hub, upper, (shard + chunks[c][0]) % shards, side]
        return jnp.concatenate([jnp.stack([v.astype(jnp.int32) for v in head]), slot_clusters])

    def merge(c, side, got, planes, held, after=()):
        j, r = chunks[c]
        weights, hiddens = [], []
        for table in (own, far):
            slots, row = table[c]
            weights += [(slot, row, 0 if j else every) for slot in slots]
            slots, row = table[r]
            hiddens += [(slot, row) for slot in slots]
        chunk = dict(weights=weights, hiddens=hiddens)
        return merge_step(
            ids_for(c, side), scales, chunk, grads[j], size, half, got, planes, held, after
        )

    result, chain = None, None
    sent, got, leaf = {}, {}, {}
    picked, turned_ones = [], []
    waiting = []

    def pack(c):
        nonlocal chain
        later = c + lead
        source, row = own[later] if later < count else ([], 0)
        packed = pack_step(
            ids_for(c, upper), sent[c + 2], got[c + 2], source, row, size, half, peers, [chain]
        )
        chain = packed
        leaf[c] = leaf_and_hub(packed)
        if later < count:
            far[later] = ([(leaf[c], k) for k in range(peers)], 0)
        waiting.append(c)

    def pick(step):
        nonlocal chain
        lo, hi = pick_step(
            ids_for(waiting[0], upper),
            [(sent[w + 2], got[w + 2], leaf[w]) for w in waiting],
            size,
            half,
            peers,
            [chain],
        )
        chain = lo
        parts = peers // 2
        come = to_peer(hi, parts)
        held = [(lo, k) for k in range(parts)] + [(come, k) for k in range(parts)]
        picked.append((step, list(waiting), held))
        waiting.clear()

    def turn():
        step, group, held = picked.pop(0)
        come = gate(held[-1][0], [chain])
        held = held[: peers // 2] + [(come, i) for _, i in held[peers // 2 :]]
        turned_ones.append((step, group, exchange(held, bit=peers // 4)))

    def put():
        nonlocal result, chain
        _, group, held = turned_ones.pop(0)
        where = []
        for w in group:
            where.append(((shard + chunks[w][0]) % shards)[None])
            where.append(ranks * pieces + chunks[w][1])
        result, chain = place_step(
            jnp.concatenate(where).astype(jnp.int32), held, result, (depth, width), [chain]
        )

    for t in range(count + 2):
        planes = (2 if t < count else 0) * CLUSTERS + (CLUSTERS if t >= 2 else 0)
        buffer = None
        if t >= 2:
            buffer = merge(t - 2, 1 - upper, got[t - 2], planes, None, [chain])
        if t < count:
            buffer = merge(t, upper, None, planes, buffer, before[t])
        chain = sent[t] = buffer
        got[t] = hub_to_hub(buffer)
        if len(waiting) == 2:
            pick(t)
        if t >= 4:
            pack(t - 4)
        if turned_ones and turned_ones[0][0] <= t - 2:
            put()
        if picked and picked[0][0] <= t - 1:
            turn()
        j, step = t // pieces + 1, t % pieces
        if not fine:
            if j < shards:
                column_grads(j, [got[t]], [])
            continue
        if t == 0:
            pair = spread(0, 2, 4, [grad_steps[1]], [sent[0]])
            rest_cut = cut_for(0, 4, pieces, [pair[0]])
            before[1].append(rest_cut[0])
        if t == 2:
            rest = spread(0, 4, pieces, rest_cut, [sent[2]])
            cuts = cut_for(1, 0, 2, [rest[0]])
            before[3].append(cuts[0])
        if t == 3:
            for array, step in zip(column_grads(1, [sent[0]], [sent[3]]), (4, 5)):
                before[step].append(array)
        if t in (3, 5, 7):
            low, high = {3: (0, 2), 5: (2, 5), 7: (5, pieces)}[t]
            before[t + 1].append(spread(1, low, high, cuts, [sent[t]])[0])
        if t in (4, 6):
            cuts = cut_for(1, *{4: (2, 5), 6: (5, pieces)}[t], [sent[t]])
            before[t + 1].append(cuts[0])
        if t + 2 < lead:
            lift(t + 2, [lifts[t + 1][1], sent[t]])
            before[t + 1].append(lifts[t + 2][0])
    pack(count - 2)
    pack(count - 1)
    later = waiting[-2:]
    del waiting[-2:]
    if waiting:
        pick(count + 2)
    while turned_ones:
        put()
    for w in later:
        waiting.append(w)
        pick(count + 2)
        turn()
        if turned_ones:
            put()
    while picked or turned_ones:
        if picked:
            turn()
        put()
    return result[None]


def solution(mesh):
    placed = (
        P("client", None, None, "mp"),
        P("client", "mp", None),
        P("client", None, "mp", None),
        P("client", None, "mp"),
        P("client", None, "mp", None),
        P(),
    )
    return jax.shard_map(
        functools.partial(body, mesh.shape["client"], mesh.shape["mp"]),
        mesh=mesh,
        in_specs=placed,
        out_specs=P("client", "mp", None),
        check_vma=False,
    )
```

```python
import functools

import jax
import jax.numpy as jnp
from jax import lax
from jax.experimental import pallas as pl
from jax.experimental.pallas import tpu as pltpu
from jax.sharding import PartitionSpec as P

CLUSTERS = 4
EPS = 1e-06
FLOOR = 0.1
LAYERS = 4
LEAD = 7
VMEM = 48 * 1024 * 1024
F32 = jnp.float32
BF16 = jnp.bfloat16
HUB, UPPER, COLUMN, SIDE, FIRST = range(5)


def call(kernel, grid, ids, scales, in_specs, operands, out_specs, out_shape, name, cost, **kw):
    prefetch = [ids] if scales is None else [ids, scales]
    aliases = {len(prefetch) + i: o for i, o in kw.pop("aliases", {}).items()}
    return pl.pallas_call(
        kernel,
        out_shape=out_shape,
        grid_spec=pltpu.PrefetchScalarGridSpec(
            num_scalar_prefetch=len(prefetch),
            grid=grid,
            in_specs=in_specs,
            out_specs=out_specs,
            scratch_shapes=kw.pop("scratch", []),
        ),
        input_output_aliases=aliases,
        compiler_params=pltpu.CompilerParams(vmem_limit_bytes=VMEM),
        cost_estimate=pl.CostEstimate(flops=cost[0], bytes_accessed=cost[1], transcendentals=0),
        name=name,
    )(*prefetch, *operands)


def gate(value, after):
    anywhere = pl.BlockSpec(memory_space=pl.ANY)
    return pl.pallas_call(
        lambda *refs: None,
        out_shape=jax.ShapeDtypeStruct(value.shape, value.dtype),
        in_specs=[anywhere] * (1 + len(after)),
        out_specs=anywhere,
        input_output_aliases={0: 0},
        cost_estimate=pl.CostEstimate(flops=1, bytes_accessed=1, transcendentals=0),
        name="gate",
    )(value, *after)


def merge_kernel(peers, parts, final, extra, ids_ref, scale_ref, *refs):
    weights, hiddens, refs = refs[: 2 * peers], refs[2 * peers : 4 * peers], refs[4 * peers :]
    grads, refs = refs[: 2 * peers * parts], refs[2 * peers * parts :]
    got_ref = refs[0] if final else None
    out_ref, num, den = refs[-3:]

    @pl.when(ids_ref[HUB] == 1)
    def _():
        if final:
            num[...] = got_ref[:CLUSTERS].astype(F32)
            den[...] = got_ref[CLUSTERS:].astype(F32)
        else:
            num[...] = jnp.zeros_like(num)
            den[...] = jnp.zeros_like(den)
        tokens = hiddens[0].shape[1] // 4
        for slot in range(2 * peers):
            fisher = None
            for batch in range(4):
                part, start = divmod(batch * tokens, grads[0].shape[0])
                grad = jnp.dot(
                    hiddens[slot][:, batch * tokens : (batch + 1) * tokens],
                    grads[slot * parts + part][start : start + tokens, :],
                    preferred_element_type=F32,
                )
                fisher = grad * grad if fisher is None else fisher + grad * grad
            a_weight = (fisher * scale_ref[slot] + FLOOR).astype(BF16).astype(F32)
            cluster = ids_ref[FIRST + slot]
            num[cluster] += a_weight * weights[slot][...].astype(F32)
            den[cluster] += a_weight
        if final:
            out_ref[...] = (num[...] / den[...]).astype(BF16)
        else:
            out_ref[:CLUSTERS] = num[...].astype(BF16)
            out_ref[CLUSTERS:] = den[...].astype(BF16)


def merge_step(ids, scales, chunk, grads, rows, half, got, planes, held, after):
    final = got is not None
    peers = len(grads) // 2
    parts = len(grads[0])
    tokens = sum(array.shape[1] for array, _ in grads[0])
    width = 256 if half % 256 == 0 else half
    tiles = half // width
    in_specs, operands = [], []
    for (array, index), row, offset in chunk["weights"]:
        operands.append(array)
        in_specs.append(
            pl.BlockSpec(
                (None, rows, width),
                lambda g, ids, sc, i=index, row=row, first=offset // width: (
                    i,
                    row,
                    first + ids[SIDE] * tiles + g,
                ),
            )
        )
    for (array, index), row in chunk["hiddens"]:
        operands.append(array)
        in_specs.append(
            pl.BlockSpec((None, rows, tokens), lambda g, ids, sc, i=index, row=row: (i, row, 0))
        )
    for slot in grads:
        for array, index in slot:
            operands.append(array)
            in_specs.append(
                pl.BlockSpec(
                    (None, array.shape[1], width),
                    lambda g, ids, sc, index=index: (index, 0, ids[SIDE] * tiles + g),
                )
            )
    if final:
        operands.append(got)
        in_specs.append(pl.BlockSpec((2 * CLUSTERS, rows, width), lambda g, ids, sc: (0, 0, g)))
    aliases = {}
    if held is not None:
        aliases = {len(operands): 0}
        operands.append(held)
        in_specs.append(pl.BlockSpec(memory_space=pl.ANY))
    for array in after:
        operands.append(array)
        in_specs.append(pl.BlockSpec(memory_space=pl.ANY))
    if final:
        place = planes // CLUSTERS - 1
        out_spec = pl.BlockSpec((CLUSTERS, rows, width), lambda g, ids, sc: (place, 0, g))
    else:
        out_spec = pl.BlockSpec((2 * CLUSTERS, rows, width), lambda g, ids, sc: (0, 0, g))
    return call(
        functools.partial(merge_kernel, peers, parts, final, len(after)),
        (tiles,),
        ids,
        scales,
        in_specs,
        operands,
        out_spec,
        jax.ShapeDtypeStruct((planes, rows, half), BF16),
        "merge_final" if final else "merge_partial",
        (4 * peers * rows * tokens * half, 4 * peers * (rows * half + rows * tokens + tokens * half)),
        aliases=aliases,
        scratch=[pltpu.VMEM((CLUSTERS, rows, width), F32)] * 2,
    )


def planes_spec(array, rows, half):
    last = array.shape[0] // CLUSTERS - 1
    return pl.BlockSpec((CLUSTERS, rows, half), lambda *_: (last, 0, 0))


def pack_kernel(up, ids_ref, mine_ref, other_ref, *refs):
    out_ref = refs[-1]
    half = mine_ref.shape[2]
    base = out_ref.shape[2] - 2 * half

    @pl.when((ids_ref[HUB] == 1) & (ids_ref[UPPER] == 0))
    def _():
        out_ref[:CLUSTERS, :, base : base + half] = other_ref[...]
        out_ref[:CLUSTERS, :, base + half :] = mine_ref[...]

    @pl.when((ids_ref[HUB] == 1) & (ids_ref[UPPER] == 1))
    def _():
        out_ref[:CLUSTERS, :, base : base + half] = mine_ref[...]
        out_ref[:CLUSTERS, :, base + half :] = other_ref[...]

    if up:

        @pl.when(ids_ref[HUB] == 0)
        def _():
            for peer in range(up):
                out_ref[peer] = refs[peer][...]


def pack_step(ids, mine, other, source, row, rows, half, peers, after):
    in_specs = [planes_spec(mine, rows, half), planes_spec(other, rows, half)]
    operands = [mine, other]
    width = 2 * half
    for array, index in source:
        width = array.shape[2]
        in_specs.append(pl.BlockSpec((None, rows, width), lambda g, ids, i=index: (i, row, 0)))
        operands.append(array)
    shape = (max(peers, CLUSTERS), rows, width)
    in_specs += [pl.BlockSpec(memory_space=pl.ANY)] * len(after)
    operands += after
    return call(
        functools.partial(pack_kernel, len(source)),
        (1,),
        ids,
        None,
        in_specs,
        operands,
        pl.BlockSpec(shape, lambda g, ids: (0, 0, 0)),
        jax.ShapeDtypeStruct(shape, BF16),
        "pack",
        (0, 4 * shape[0] * rows * width),
    )


def pick_kernel(peers, chunks, ids_ref, *refs):
    outs = refs[-2:]
    for index in range(chunks):
        mine_ref, other_ref, leaf_ref = refs[3 * index : 3 * index + 3]
        half = mine_ref.shape[2]
        base = leaf_ref.shape[2] - 2 * half
        for peer in range(peers):
            cluster = ids_ref[FIRST + peer]
            out_ref = outs[peer // (peers // 2)]
            to = peer % (peers // 2)

            @pl.when((ids_ref[HUB] == 1) & (ids_ref[UPPER] == 0))
            def _():
                out_ref[to, index, :, :half] = other_ref[cluster]
                out_ref[to, index, :, half:] = mine_ref[cluster]

            @pl.when((ids_ref[HUB] == 1) & (ids_ref[UPPER] == 1))
            def _():
                out_ref[to, index, :, :half] = mine_ref[cluster]
                out_ref[to, index, :, half:] = other_ref[cluster]

            @pl.when(ids_ref[HUB] == 0)
            def _():
                out_ref[to, index] = leaf_ref[cluster, :, base:]


def pick_step(ids, group, rows, half, peers, after):
    in_specs, operands = [], []
    for mine, other, leaf in group:
        operands += [mine, other, leaf]
        in_specs += [planes_spec(mine, rows, half), planes_spec(other, rows, half)]
        in_specs.append(pl.BlockSpec(leaf.shape, lambda *_: (0, 0, 0)))
    shape = (peers // 2, len(group), rows, 2 * half)
    in_specs += [pl.BlockSpec(memory_space=pl.ANY)] * len(after)
    operands += after
    return call(
        functools.partial(pick_kernel, peers, len(group)),
        (1,),
        ids,
        None,
        in_specs,
        operands,
        [pl.BlockSpec(shape, lambda g, ids: (0, 0, 0, 0))] * 2,
        [jax.ShapeDtypeStruct(shape, BF16)] * 2,
        "pick",
        (0, 16 * rows * half * len(group) * peers),
    )


def place_kernel(peers, ids_ref, *refs):
    out_ref, token_ref = refs[-2:]
    token_ref[...] = jnp.zeros_like(token_ref)
    for peer in range(peers):

        @pl.when(pl.program_id(1) == peer)
        def _(peer=peer):
            out_ref[...] = refs[peer][...]


def place_step(ids, blocks, result, shape, after):
    peers = len(blocks)
    _, chunks, rows, width = blocks[0][0].shape
    step = 1 + peers
    in_specs = [
        pl.BlockSpec((None, None, rows, width), lambda c, p, ids, i=index: (i, c, 0, 0))
        for _, index in blocks
    ]
    return call(
        functools.partial(place_kernel, peers),
        (chunks, peers),
        ids,
        None,
        in_specs + [pl.BlockSpec(memory_space=pl.ANY)] * (len(after) + (result is not None)),
        [array for array, _ in blocks] + [result] * (result is not None) + after,
        [
            pl.BlockSpec((rows, width), lambda c, p, ids: (ids[c * step + 1 + p], ids[c * step])),
            pl.BlockSpec((8, 128), lambda c, p, ids: (0, 0)),
        ],
        [jax.ShapeDtypeStruct(shape, BF16), jax.ShapeDtypeStruct((8, 128), F32)],
        "place",
        (0, 4 * chunks * peers * rows * width),
        aliases={peers: 0} if result is not None else {},
    )


def forward_kernel(own, batches, ids_ref, hidden_ref, weight_ref, target_ref, *refs):
    outs = refs[-1:] if own else refs[-2:]
    total = jnp.dot(hidden_ref[...], weight_ref[...], preferred_element_type=F32)
    tokens = hidden_ref.shape[0] // batches
    span = target_ref.shape[1]
    outs[0][...] = total
    for batch in range(batches):
        rows = pl.ds(pl.multiple_of(batch * tokens + ids_ref[0] * span, 8), span)
        outs[0][rows, :] = outs[0][rows, :] - target_ref[batch].astype(F32)
    if not own:

        @pl.when(pl.program_id(0) == 0)
        def _():
            for batch in range(batches):
                rows = hidden_ref[batch * tokens : (batch + 1) * tokens, :]
                outs[1][batch] = lax.dot_general(
                    rows, rows, (((1,), (1,)), ((), ())), preferred_element_type=F32
                )


def forward_step(ids, flat, weight, target, block, shards, own, after=()):
    every, depth = flat.shape
    batches = target.shape[0]
    tokens = every // batches
    width = min(block, 256)
    tiles = block // width
    count = tiles if own else tiles * (shards - 1)
    columns = lambda g, ids: ids[1 + g // tiles] * tiles + g % tiles
    out_specs = [pl.BlockSpec((every, width), lambda g, ids: (0, g))]
    out_shape = [jax.ShapeDtypeStruct((every, count * width), F32)]
    if not own:
        out_specs.append(pl.BlockSpec((batches, tokens, tokens), lambda g, ids: (0, 0, 0)))
        out_shape.append(jax.ShapeDtypeStruct((batches, tokens, tokens), F32))
    return call(
        functools.partial(forward_kernel, own, batches),
        (count,),
        ids.astype(jnp.int32),
        None,
        [
            pl.BlockSpec((every, depth), lambda g, ids: (0, 0)),
            pl.BlockSpec((depth, width), lambda g, ids: (0, columns(g, ids))),
            pl.BlockSpec((batches, target.shape[1], width), lambda g, ids: (0, 0, columns(g, ids))),
        ]
        + [pl.BlockSpec(memory_space=pl.ANY)] * len(after),
        [flat, weight, target, *after],
        out_specs,
        out_shape,
        "forward",
        (1, 1),
    )


def grad_kernel(batches, ids_ref, token_ref, gram_ref, mine_ref, *refs):
    grad_ref, total_ref = refs[-2:]
    total = mine_ref[...]
    for ref in refs[:-2]:
        total = total + ref[...]
    grad_ref[...] = (token_ref[...] * total).astype(BF16)
    tokens = grad_ref.shape[0] // batches
    squares = 0.0
    for batch in range(batches):
        rows = grad_ref[batch * tokens : (batch + 1) * tokens, :]
        gram = lax.dot_general(rows, rows, (((1,), (1,)), ((), ())), preferred_element_type=F32)
        squares = squares + jnp.sum(gram_ref[batch] * gram)
    total_ref[...] = jnp.full(total_ref.shape, squares, F32)


def grad_step(ids, token_weight, hidden_gram, mine, others):
    arrays = [token_weight, hidden_gram, mine, *others]
    whole = lambda a: pl.BlockSpec(a.shape, lambda *_: (0,) * a.ndim)
    outs = [jax.ShapeDtypeStruct(mine.shape, BF16), jax.ShapeDtypeStruct((8, 128), F32)]
    return call(
        functools.partial(grad_kernel, hidden_gram.shape[0]),
        (1,),
        ids.astype(jnp.int32),
        None,
        [whole(a) for a in arrays],
        arrays,
        [whole(a) for a in outs],
        outs,
        "grad",
        (1, 1),
    )


def cut_kernel(count, every, ids_ref, weight_ref, *refs):
    outs = refs[-2:]
    for index in range(2):

        @pl.when(pl.program_id(0) // count == index)
        def _(index=index):
            if every:
                outs[index][:, :every] = refs[0][...]
            outs[index][:, every:] = weight_ref[...]


def cut_step(ids, weight, turned, size, chunks, block, peers, after):
    count = peers // 2
    in_specs = [pl.BlockSpec((size, block), lambda p, c, ids: (ids[1 + p] + c, ids[0]))]
    operands = [weight]
    every = 0
    if turned is not None:
        every = turned.shape[1]
        in_specs.append(pl.BlockSpec((size, every), lambda p, c, ids: (ids[1 + p] + c, 0)))
        operands.append(turned)
    for array in after:
        operands.append(array)
        in_specs.append(pl.BlockSpec(memory_space=pl.ANY))
    shape = (count, chunks * size, every + block)
    spec = lambda index: pl.BlockSpec((None, size, every + block), index)
    return call(
        functools.partial(cut_kernel, count, every),
        (peers, chunks),
        ids,
        None,
        in_specs,
        operands,
        [
            spec(lambda p, c, ids: (jnp.minimum(p, count - 1), jnp.where(p < count, c, chunks - 1), 0)),
            spec(lambda p, c, ids: (jnp.maximum(p - count, 0), jnp.where(p < count, 0, c), 0)),
        ],
        [jax.ShapeDtypeStruct(shape, BF16)] * 2,
        "cut",
        (1, 1),
    )


def body(clients, shards, hidden, weight, target, router_prob, routes, assign):
    batches, tokens, depth = hidden.shape[1:]
    width = weight.shape[2]
    peers = clients // LAYERS
    rows = depth // peers
    block = width // shards
    half = block // 2
    pieces = max(1, 14 // shards)
    if rows % (16 * pieces):
        pieces = 1
    size = rows // pieces
    every = batches * tokens
    chunks = [(j, r) for j in range(shards) for r in range(pieces)]
    count = len(chunks)
    lead = min(LEAD, count)

    client = lax.axis_index("client")
    shard = lax.axis_index("mp")
    layer, place = client // peers, client % peers
    is_hub = (layer == 1) | (layer == 2)
    upper = (layer >= 2).astype(jnp.int32)
    ranks = place ^ jnp.arange(peers)

    def swap(k):
        return [(z * peers + q, z * peers + (q ^ k)) for z in range(LAYERS) for q in range(peers)]

    def between(links):
        return [(a * peers + q, b * peers + q) for a, b in links for q in range(peers)]

    to_peer = lambda array, k: lax.ppermute(array, "client", swap(k))
    leaf_to_hub = lambda array: lax.ppermute(array, "client", between([(0, 1), (3, 2)]))
    leaf_and_hub = lambda array: lax.ppermute(
        array, "client", between([(0, 1), (1, 0), (2, 3), (3, 2)])
    )
    hub_to_hub = lambda array: lax.ppermute(array, "client", between([(1, 2), (2, 1)]))
    ahead = lambda j: [(s, (s + j) % shards) for s in range(shards)]
    behind = lambda j: [(s, (s - j) % shards) for s in range(shards)]

    def exchange(held, after=(), bit=peers // 2):
        held = list(held)
        while bit:
            moved = [k for k in range(peers) if k & bit]
            arrays = {id(held[k][0]) for k in moved}
            if len(arrays) == 1 and held[moved[0]][0].shape[0] == len(moved):
                array = held[moved[0]][0]
            else:
                array = jnp.stack([held[k][0][held[k][1]] for k in moved])
            got = to_peer(array, bit)
            if after and bit == peers // 2:
                got = gate(got, after)
            for i, k in enumerate(moved):
                held[k] = (got, i)
            bit //= 2
        return held

    def gather_pair(near, distant, after, last=()):
        top = peers // 2
        near_top = to_peer(near[None], top)
        distant = gate(distant, [near_top, *after])
        distant_top = to_peer(distant[None], top)
        distant_top = gate(distant_top, last) if last else distant_top
        held = [
            {0: (near[None], 0), top: (near_top, 0)},
            {0: (distant[None], 0), top: (distant_top, 0)},
        ]
        bit = top // 2
        while bit:
            keys = [(n, k) for n in range(2) for k in held[n]]
            stack = jnp.stack([held[n][k][0][held[n][k][1]] for n, k in keys])
            got = to_peer(stack, bit)
            for i, (n, k) in enumerate(keys):
                held[n][k] = (stack, i)
                held[n][k ^ bit] = (got, i)
            bit //= 2
        slots = [h[k] for h in held for k in range(peers)]
        return slots, near_top, distant_top, stack, got

    local_weight = weight[0]
    flat = hidden[0].reshape(every, depth)
    turned = flat.T
    others_at = jnp.concatenate([shard[None], (shard + jnp.arange(1, shards)) % shards])
    others, hidden_gram = forward_step(others_at, flat, local_weight, target[0], block, shards, False)
    own_gram = hidden_gram
    for j in range(1, shards):
        hidden_gram = hidden_gram + lax.ppermute(own_gram, "mp", ahead(j))

    def cut_for(j, low, high, after):
        order = [place ^ (k + peers // 2) % peers for k in range(peers)]
        at = jnp.stack([(shard + j) % shards] + [q * pieces + low for q in order]).astype(jnp.int32)
        return tuple(
            cut_step(at, local_weight, None if j else turned, size, high - low, block, peers, after)
        )

    def spread(j, low, high, after, later=()):
        hi, lo = after if type(after) is tuple else cut_for(j, low, high, after)
        parts = peers // 2
        held = exchange([((lo, hi)[k // parts], k % parts) for k in range(peers)], later)
        numbers = [j * pieces + r for r in range(low, high)]
        for i, c in enumerate(numbers):
            own[c] = (held, i)
        return held[parts][0], held[-1][0], hi

    def lift(c, after=()):
        held, row = own[c]
        array = jnp.stack([a[i, row * size : (row + 1) * size] for a, i in held])
        array = gate(array, after) if after else array
        lifts[c] = array, leaf_to_hub(array)
        far[c] = ([(lifts[c][1], k) for k in range(peers)], 0)

    lifts = {}
    own, far = {}, {}
    fine = pieces >= 7
    early = [spread(0, 0, 1 if fine else pieces, [others])]
    if fine:
        early.append(spread(0, 1, 2, [early[0][2]]))
    mine_at = jnp.stack([shard, shard])
    (mine,) = forward_step(
        mine_at, flat, local_weight, target[0], block, shards, True, [e[2] for e in early]
    )
    token_weight = jnp.where(jnp.any(routes[0] == 0, axis=-1), router_prob[0], 0.0)
    token_weight = jnp.stack(
        [token_weight] + [lax.ppermute(token_weight, "mp", behind(j)) for j in range(1, shards)]
    )
    token_weight = token_weight[(jnp.arange(shards) - shard) % shards]
    token_weight = token_weight.transpose(1, 0, 2).reshape(every, 1)
    arrived = [
        lax.ppermute(others[:, (j - 1) * block : j * block], "mp", ahead(j)) for j in range(1, shards)
    ]
    grad, squares = grad_step(
        mine_at, token_weight, hidden_gram, gate(mine, [early[-1][0]]), arrived
    )
    total = squares
    for j in range(1, shards):
        total = total + lax.ppermute(squares, "mp", ahead(j))
    leaf_total = leaf_to_hub(total)
    totals, *scalar_steps = gather_pair(total, leaf_total, [])
    totals = jnp.stack([a[i, 0, 0] for a, i in totals])
    scales = 1.0 / (totals / (depth * shards * width) + EPS)
    leaf_grad = leaf_to_hub(grad)
    lift(0, [leaf_grad, leaf_total])
    grad_slots, *grad_steps = gather_pair(
        grad, leaf_grad, [scalar_steps[1], early[0][1], early[-1][1]], [lifts[0][1]]
    )

    grads = {0: [[slot] for slot in grad_slots]}

    cluster_of = assign[:, 0].astype(jnp.int32)
    slot_clients = jnp.concatenate(
        [layer * peers + ranks, jnp.where(upper == 1, 3, 0) * peers + ranks]
    )
    slot_clusters = cluster_of[slot_clients]

    before = {t: [] for t in range(count)}

    def column_grads(j, first_after, second_after):
        first, second = grad_steps[2:]
        come = lax.ppermute(gate(first, first_after), "mp", behind(j))
        ready = gate(second, [come, *second_after])
        pair = come, lax.ppermute(ready, "mp", behind(j))
        grads[j] = [[(pair[0] if a is first else pair[1], i)] for a, i in grad_slots]
        return come, ready

    if fine:
        lift(1, [lifts[0][1]])
        before[0].append(lifts[1][1])
    else:
        last = early[0]
        for j in range(1, shards):
            last = spread(j, 0, pieces, [last[1]])
        for c in range(1, lead):
            lift(c)

    def ids_for(c, side):
        head = [is_hub, upper, (shard + chunks[c][0]) % shards, side]
        return jnp.concatenate([jnp.stack([v.astype(jnp.int32) for v in head]), slot_clusters])

    def merge(c, side, got, planes, held, after=()):
        j, r = chunks[c]
        weights, hiddens = [], []
        for table in (own, far):
            slots, row = table[c]
            weights += [(slot, row, 0 if j else every) for slot in slots]
            slots, row = table[r]
            hiddens += [(slot, row) for slot in slots]
        chunk = dict(weights=weights, hiddens=hiddens)
        return merge_step(
            ids_for(c, side), scales, chunk, grads[j], size, half, got, planes, held, after
        )

    result, chain = None, None
    sent, got, leaf = {}, {}, {}
    picked, turned_ones = [], []
    waiting = []

    def pack(c):
        nonlocal chain
        later = c + lead
        source, row = own[later] if later < count else ([], 0)
        packed = pack_step(
            ids_for(c, upper), sent[c + 2], got[c + 2], source, row, size, half, peers, [chain]
        )
        chain = packed
        leaf[c] = leaf_and_hub(packed)
        if later < count:
            far[later] = ([(leaf[c], k) for k in range(peers)], 0)
        waiting.append(c)

    def pick(step):
        nonlocal chain
        lo, hi = pick_step(
            ids_for(waiting[0], upper),
            [(sent[w + 2], got[w + 2], leaf[w]) for w in waiting],
            size,
            half,
            peers,
            [chain],
        )
        chain = lo
        parts = peers // 2
        come = to_peer(hi, parts)
        held = [(lo, k) for k in range(parts)] + [(come, k) for k in range(parts)]
        picked.append((step, list(waiting), held))
        waiting.clear()

    def turn():
        step, group, held = picked.pop(0)
        come = gate(held[-1][0], [chain])
        held = held[: peers // 2] + [(come, i) for _, i in held[peers // 2 :]]
        turned_ones.append((step, group, exchange(held, bit=peers // 4)))

    def put():
        nonlocal result, chain
        _, group, held = turned_ones.pop(0)
        where = []
        for w in group:
            where.append(((shard + chunks[w][0]) % shards)[None])
            where.append(ranks * pieces + chunks[w][1])
        result, chain = place_step(
            jnp.concatenate(where).astype(jnp.int32), held, result, (depth, width), [chain]
        )

    for t in range(count + 2):
        planes = (2 if t < count else 0) * CLUSTERS + (CLUSTERS if t >= 2 else 0)
        buffer = None
        if t >= 2:
            buffer = merge(t - 2, 1 - upper, got[t - 2], planes, None, [chain])
        if t < count:
            buffer = merge(t, upper, None, planes, buffer, before[t])
        chain = sent[t] = buffer
        got[t] = hub_to_hub(buffer)
        if fine and t < 2:
            before[t + 1].append(got[t])
        if len(waiting) == 2:
            pick(t)
        if t >= 4:
            pack(t - 4)
        if turned_ones and turned_ones[0][0] <= t - 2:
            put()
        if picked and picked[0][0] <= t - 1:
            turn()
        j, step = t // pieces + 1, t % pieces
        if not fine:
            if j < shards:
                column_grads(j, [got[t]], [])
            continue
        if t == 0:
            pair = spread(0, 2, 4, [grad_steps[1]], [sent[0]])
            rest_cut = cut_for(0, 4, pieces, [pair[0]])
            before[1].append(rest_cut[0])
        if t == 2:
            rest = spread(0, 4, pieces, rest_cut, [sent[2]])
            cuts = cut_for(1, 0, 2, [rest[0]])
            before[3].append(cuts[0])
        if t == 3:
            for array, step in zip(column_grads(1, [sent[0]], [sent[3]]), (4, 5)):
                before[step].append(array)
        if t in (3, 5, 7):
            low, high = {3: (0, 2), 5: (2, 5), 7: (5, pieces)}[t]
            before[t + 1].append(spread(1, low, high, cuts, [sent[t]])[0])
        if t in (4, 6):
            cuts = cut_for(1, *{4: (2, 5), 6: (5, pieces)}[t], [sent[t]])
            before[t + 1].append(cuts[0])
        if t + 2 < lead:
            lift(t + 2, [lifts[t + 1][1], sent[t]])
            before[t + 1].append(lifts[t + 2][0])
    pack(count - 2)
    pack(count - 1)
    later = waiting[-2:]
    del waiting[-2:]
    if waiting:
        pick(count + 2)
    while turned_ones:
        put()
    for w in later:
        waiting.append(w)
        pick(count + 2)
        turn()
        if turned_ones:
            put()
    while picked or turned_ones:
        if picked:
            turn()
        put()
    return result[None]


def solution(mesh):
    placed = (
        P("client", None, None, "mp"),
        P("client", "mp", None),
        P("client", None, "mp", None),
        P("client", None, "mp"),
        P("client", None, "mp", None),
        P(),
    )
    return jax.shard_map(
        functools.partial(body, mesh.shape["client"], mesh.shape["mp"]),
        mesh=mesh,
        in_specs=placed,
        out_specs=P("client", "mp", None),
        check_vma=False,
    )
```
